256 devices in a mesh: pipe: 16 (over y, z_hi, core), expert: 16 (over x, z_lo).
Axes of the slice: x: 4, y: 4, z: 8 (z_hi: 2, z_lo: 4; z = z_hi * 4 + z_lo), core: 2. Of those that a mesh axis runs over, the one named last changes fastest.
Arguments:
- forward_layer_input: bfloat16 [32768, 3584], P(('pipe', 'expert')), may hold values from -6 to 6
- front_ids: int32 [32768, 8], P(('pipe', 'expert')), may hold values from 0 to 255, as said below
- front_gate: bfloat16 [32768, 8], P(('pipe', 'expert')), may hold values from 0.19921875 to 1.5
- forward_norm_gain: float32 [16, 3584], P('pipe'), may hold values from 0.5 to 1.5
- front_w_in: bfloat16 [16, 2, 3584, 2048], P('pipe', None, None, 'expert'), may hold values from -0.09375 to 0.09375
- front_w_down: bfloat16 [16, 2048, 3584], P('pipe', 'expert'), may hold values from -0.1875 to 0.1875
- backward_saved_input: bfloat16 [32768, 3584], P(('pipe', 'expert')), may hold values from -6 to 6
- back_grad: bfloat16 [32768, 3584], P(('pipe', 'expert')), may hold values from -6 to 6
- back_ids: int32 [32768, 8], P(('pipe', 'expert')), may hold values from 0 to 255, as said below
- back_gate: bfloat16 [32768, 8], P(('pipe', 'expert')), may hold values from 0.19921875 to 1.5
- backward_norm_gain: float32 [16, 3584], P('pipe'), may hold values from 0.5 to 1.5
- back_w_in: bfloat16 [16, 2, 3584, 2048], P('pipe', None, None, 'expert'), may hold values from -0.09375 to 0.09375
- back_w_down: bfloat16 [16, 2048, 3584], P('pipe', 'expert'), may hold values from -0.1875 to 0.1875
Outputs:
- next_input: bfloat16 [32768, 3584], P(('pipe', 'expert'))
- next_grad: bfloat16 [32768, 3584], P(('pipe', 'expert'))
The draws below stay inside these ranges and needn't reach their ends.
Inputs may be any that keep to these rules, and one draw needn't show every extreme that they name: `front_ids`: each row names 8 different experts. Experts 0 to 1 are the section's experts computed here. In the 128 rows of one device each of them is named by at most 32 rows, and in every draw some section has one of them named by exactly 32 rows on every device of that section. `back_ids`: as for front_ids.
All inputs are finite; a program needn't handle non-finite values.
Results may differ from the reference program's by a relative error of at most 0.0055.
Values may be sent and summed in bfloat16 or wider, within the bound.
A program may use at most 128 MiB of HBM per device.

```python
import jax
import jax.numpy as jnp
from jax import lax

D = 3584
FF_WIN = 1024
NUM_EXPERTS = 256
TOPK = 8
EXP_WIN = 2
TOK = 128
CAP = 32
HID_DEV = 128
TOKENS = 32768
N_PIPE = 16
N_EXPERT = 16


def window_ids(key):
    blocks = TOKENS // TOK
    per_section = blocks // N_PIPE
    keys = jax.random.split(key, 8)
    counts = jax.random.randint(keys[0], (blocks, EXP_WIN), CAP // 4, CAP + 1)
    section = jax.random.randint(keys[1], (), 0, N_PIPE)
    which = jax.random.randint(keys[2], (), 0, EXP_WIN)
    full = (jnp.arange(blocks) // per_section == section)[:, None] & (jnp.arange(EXP_WIN) == which)[None, :]
    counts = jnp.where(full, CAP, counts)
    perm_keys = jax.random.split(keys[3], blocks * EXP_WIN)
    perms = jax.vmap(lambda one: jax.random.permutation(one, TOK))(perm_keys).reshape(blocks, EXP_WIN, TOK)
    member = perms < counts[:, :, None]
    others_count = NUM_EXPERTS - EXP_WIN
    base = jax.random.randint(keys[4], (blocks, TOK), 0, others_count)
    stride = jax.random.randint(keys[5], (blocks, TOK), 1, 32)
    positions = jnp.arange(TOPK)
    others = EXP_WIN + (base[..., None] + stride[..., None] * positions) % others_count
    slot_first = jax.random.randint(keys[6], (blocks, TOK), 0, TOPK)
    slot_second = (slot_first + 1 + jax.random.randint(keys[7], (blocks, TOK), 0, TOPK - 1)) % TOPK
    chosen = jnp.where((positions == slot_first[..., None]) & member[:, 0][..., None], 0, others)
    chosen = jnp.where((positions == slot_second[..., None]) & member[:, 1][..., None], 1, chosen)
    return chosen.reshape(TOKENS, TOPK).astype(jnp.int32)


def draw_front_ids(key, part):
    key = jax.random.fold_in(key, 11)
    return window_ids(key)


def draw_back_ids(key, part):
    key = jax.random.fold_in(key, 12)
    return window_ids(key)


def steps_of(own_key, dims, cuts, smallest, high):
    factor_of, own = 1.0, jax.random.fold_in(own_key, 6)
    for dim, parts in cuts:
        draws = jnp.exp(jax.random.uniform(jax.random.fold_in(own, dim), (parts,), jnp.float32, smallest / len(cuts), high / len(cuts)))
        factor_of = factor_of * jnp.repeat(draws, dims[dim] // parts).reshape([-1 if axis == dim else 1 for axis in range(len(dims))])
    return factor_of


def normal_values(stream_key, shape, spread, reach, cuts=(), kind=jnp.bfloat16):
    entries = jax.random.normal(stream_key, shape, jnp.float32) * spread
    if len(cuts) > 0:
        entries = steps_of(stream_key, shape, cuts, -0.22, 0.18) * entries
    return jnp.clip(entries, min=-reach, max=reach).astype(kind)


def setup_inputs(seed: int = 0) -> dict:
    arg_keys = jax.random.split(jax.random.key(seed), 14)
    forward_layer_input = normal_values(arg_keys[0], (TOKENS, D), 1.0, 6.0, ((0, 256),))
    front_ids = draw_front_ids(jax.random.fold_in(arg_keys[13], 71), 0)
    front_gate = jnp.clip(0.19921875 + 1.3007812 * jax.random.uniform(arg_keys[2], (TOKENS, TOPK), jnp.float32) ** steps_of(arg_keys[2], (TOKENS, TOPK), ((0, 256),), -0.2, 0.2), 0.19921875, 1.5).astype(jnp.bfloat16)
    forward_norm_gain = jnp.clip(1.0 + 0.1 * jax.random.normal(arg_keys[3], (N_PIPE, D), jnp.float32), 0.5, 1.5)
    front_w_in = normal_values(arg_keys[4], (N_PIPE, 2, D, EXP_WIN * FF_WIN), D ** -0.5, 0.09375, ((0, 16), (3, 16)))
    front_w_down = normal_values(arg_keys[5], (N_PIPE, EXP_WIN * FF_WIN, D), FF_WIN ** -0.5, 0.1875, ((0, 16), (1, 16)))
    backward_saved_input = normal_values(arg_keys[6], (TOKENS, D), 1.0, 6.0, ((0, 256),))
    back_grad = normal_values(arg_keys[7], (TOKENS, D), 1.0, 6.0, ((0, 256),))
    back_ids = draw_back_ids(jax.random.fold_in(arg_keys[13], 71), 0)
    back_gate = jnp.clip(0.19921875 + 1.3007812 * jax.random.uniform(arg_keys[9], (TOKENS, TOPK), jnp.float32) ** steps_of(arg_keys[9], (TOKENS, TOPK), ((0, 256),), -0.2, 0.2), 0.19921875, 1.5).astype(jnp.bfloat16)
    backward_norm_gain = jnp.clip(1.0 + 0.1 * jax.random.normal(arg_keys[10], (N_PIPE, D), jnp.float32), 0.5, 1.5)
    back_w_in = normal_values(arg_keys[11], (N_PIPE, 2, D, EXP_WIN * FF_WIN), D ** -0.5, 0.09375, ((0, 16), (3, 16)))
    back_w_down = normal_values(arg_keys[12], (N_PIPE, EXP_WIN * FF_WIN, D), FF_WIN ** -0.5, 0.1875, ((0, 16), (1, 16)))
    return {"forward_layer_input": forward_layer_input, "front_ids": front_ids, "front_gate": front_gate, "forward_norm_gain": forward_norm_gain, "front_w_in": front_w_in, "front_w_down": front_w_down, "backward_saved_input": backward_saved_input, "back_grad": back_grad, "back_ids": back_ids, "back_gate": back_gate, "backward_norm_gain": backward_norm_gain, "back_w_in": back_w_in, "back_w_down": back_w_down}


EPS = 1e-06

def slot_tables(expert_ids, route_gate):
    labels = jnp.arange(EXP_WIN, dtype=jnp.int32)
    match = expert_ids[None, :, :] == labels[:, None, None]
    chosen = jnp.any(match, axis=2)
    weights = lax.optimization_barrier(jnp.sum(jnp.where(match, route_gate.astype(jnp.float32)[None], jnp.float32(0.0)), axis=2))
    place = jnp.cumsum(chosen.astype(jnp.int32), axis=1) - 1
    slots = jnp.arange(CAP, dtype=jnp.int32)
    table = chosen[:, None, :] & (place[:, None, :] == slots[None, :, None])
    forward_route_table = table.astype(jnp.float32)
    slot_gate = lax.optimization_barrier(jnp.sum(forward_route_table * weights[:, None, :], axis=2))
    return (forward_route_table, slot_gate.astype(jnp.bfloat16))

def apply_rms_norm(layer_in, gain):
    values = layer_in.astype(jnp.float32)
    scale = lax.rsqrt(lax.optimization_barrier(jnp.mean(values * values, axis=-1, keepdims=True)) + EPS)
    return (values, scale, (values * scale * gain).astype(jnp.bfloat16))

def times_transposed(left, right):
    return lax.dot_general(left, right, (((1,), (1,)), ((), ())), preferred_element_type=jnp.float32)

def expert_forward(slot_x, slot_g, w_in, w_down):
    shape = slot_x.shape
    flat = slot_x.reshape(-1, shape[-1])
    gate_pre = jnp.dot(flat, w_in[0], preferred_element_type=jnp.float32)
    up_pre = jnp.dot(flat, w_in[1], preferred_element_type=jnp.float32)
    hidden = (jax.nn.silu(gate_pre) * up_pre * slot_g.reshape(-1, 1).astype(jnp.float32)).astype(jnp.bfloat16)
    part = jnp.dot(hidden, w_down, preferred_element_type=jnp.float32).astype(jnp.bfloat16)
    return part.reshape(shape)

def expert_backward(slot_x, slot_dy, slot_g, w_in, w_down):
    shape = slot_x.shape
    flat = slot_x.reshape(-1, shape[-1])
    gate_pre = jnp.dot(flat, w_in[0], preferred_element_type=jnp.float32)
    up_pre = jnp.dot(flat, w_in[1], preferred_element_type=jnp.float32)
    grad_h = times_transposed(slot_dy.reshape(-1, shape[-1]), w_down) * slot_g.reshape(-1, 1).astype(jnp.float32)
    sig = jax.nn.sigmoid(gate_pre)
    grad_gate = (grad_h * up_pre * sig * (1.0 + gate_pre * (1.0 - sig))).astype(jnp.bfloat16)
    grad_up = (grad_h * gate_pre * sig).astype(jnp.bfloat16)
    part = times_transposed(grad_gate, w_in[0]) + times_transposed(grad_up, w_in[1])
    return part.astype(jnp.bfloat16).reshape(shape)

def gather_into_slots(tables, rows):
    return jnp.einsum('secr,srd->secd', tables, rows.astype(jnp.float32)).astype(jnp.bfloat16)

def one_section(args):
    forward_activation, ids_f, gate_f, forward_gain_vector, win_f, wdown_f, backward_activation, dy_b, ids_b, gate_b, backward_gain_vector, win_b, wdown_b = args
    hidden_partition = N_EXPERT // EXP_WIN
    forward_route_tables, sgate_f = jax.vmap(slot_tables)(ids_f, gate_f)
    forward_float_input, forward_inverse_scale, forward_normalized = apply_rms_norm(forward_activation, forward_gain_vector)
    delivered_forward = gather_into_slots(forward_route_tables, forward_normalized)
    backward_route_tables, sgate_b = jax.vmap(slot_tables)(ids_b, gate_b)
    backward_float_input, backward_inverse_scale, backward_normalized = apply_rms_norm(backward_activation, backward_gain_vector)
    delivered_backward = gather_into_slots(backward_route_tables, backward_normalized)
    sent_dy = gather_into_slots(backward_route_tables, dy_b)

    def fwd_device(index):
        which = index // hidden_partition
        slot_x = lax.dynamic_index_in_dim(delivered_forward, which, 1, keepdims=False)
        slot_g = lax.dynamic_index_in_dim(sgate_f, which, 1, keepdims=False)
        w_in = lax.dynamic_slice_in_dim(win_f, index * HID_DEV, HID_DEV, 2)
        w_down = lax.dynamic_slice_in_dim(wdown_f, index * HID_DEV, HID_DEV, 0)
        return expert_forward(slot_x, slot_g, w_in, w_down)

    def bwd_device(index):
        which = index // hidden_partition
        slot_x = lax.dynamic_index_in_dim(delivered_backward, which, 1, keepdims=False)
        slot_dy = lax.dynamic_index_in_dim(sent_dy, which, 1, keepdims=False)
        slot_g = lax.dynamic_index_in_dim(sgate_b, which, 1, keepdims=False)
        w_in = lax.dynamic_slice_in_dim(win_b, index * HID_DEV, HID_DEV, 2)
        w_down = lax.dynamic_slice_in_dim(wdown_b, index * HID_DEV, HID_DEV, 0)
        return expert_backward(slot_x, slot_dy, slot_g, w_in, w_down)
    devices = jnp.arange(N_EXPERT, dtype=jnp.int32)
    parts_f = lax.map(fwd_device, devices)
    parts_b = lax.map(bwd_device, devices)
    total_f = parts_f.astype(jnp.float32).reshape((EXP_WIN, hidden_partition) + parts_f.shape[1:]).sum(axis=1)
    total_b = parts_b.astype(jnp.float32).reshape((EXP_WIN, hidden_partition) + parts_b.shape[1:]).sum(axis=1)
    moe_f = jnp.einsum('secr,escd->srd', forward_route_tables, total_f, precision=lax.Precision.HIGHEST)
    moe_b = jnp.einsum('secr,escd->srd', backward_route_tables, total_b, precision=lax.Precision.HIGHEST)
    out_f = (forward_float_input + moe_f).astype(jnp.bfloat16)
    dyf = dy_b.astype(jnp.float32)
    grad_x = dyf + backward_inverse_scale * backward_gain_vector * moe_b - backward_float_input * (backward_inverse_scale * backward_inverse_scale * backward_inverse_scale) * lax.optimization_barrier(jnp.mean(backward_float_input * backward_gain_vector * moe_b, axis=-1, keepdims=True))
    return (out_f, grad_x.astype(jnp.bfloat16))

def reference(forward_layer_input, front_ids, front_gate, forward_norm_gain, front_w_in, front_w_down, backward_saved_input, back_grad, back_ids, back_gate, backward_norm_gain, back_w_in, back_w_down):

    def view(array):
        return array.reshape((N_PIPE, N_EXPERT, TOK) + array.shape[1:])
    stacked = (view(forward_layer_input), view(front_ids), view(front_gate), forward_norm_gain, front_w_in, front_w_down, view(backward_saved_input), view(back_grad), view(back_ids), view(back_gate), backward_norm_gain, back_w_in, back_w_down)
    outs_f, outs_b = lax.map(one_section, stacked)
    next_input = jnp.concatenate([jnp.zeros_like(outs_f[:1]), outs_f[:-1]], axis=0)
    next_grad = jnp.concatenate([jnp.zeros_like(outs_b[:1]), outs_b[:-1]], axis=0)
    return (next_input.reshape(TOKENS, D), next_grad.reshape(TOKENS, D))
```

```python
import functools

import jax
import jax.numpy as jnp
from jax import lax
from jax.experimental import pallas as pl
from jax.experimental.pallas import tpu as pltpu
from jax.sharding import PartitionSpec as P

MESH = pl.DeviceIdType.MESH
F32 = jnp.float32
BF16 = jnp.bfloat16

D = 3584
CAP = 32
TOK = 128
HID = 128
NZ = 4
NC = 7
CW = D // NC
KC = 896
EPS = 1e-06


def dot(a, b):
    return jnp.dot(a, b, preferred_element_type=F32)


def dot_t(a, b):
    return lax.dot_general(a, b, (((1,), (1,)), ((), ())), preferred_element_type=F32)


def kernel(
    x_ref, idf_ref, gf_ref, gainf_ref, winf_ref, wdf_ref,
    xb_ref, dy_ref, idb_ref, gb_ref, gainb_ref, winb_ref, wdb_ref,
    outf_ref, outb_ref,
    xf_v, xb_v, dy_v, xh, rinv, tg_f, tg_b,
    wgu_b, wd_b, wgu_f, wd_f,
    g_b, g_f, x_b, x_f, p_b, p_f, r_b, r_f, tot_b, tot_f,
    acc, accd, hid, moe, o_b, o_f, zero,
    lsem, ws, wr, gs_b, gr_b, gs_f, gr_f, xs, rs_b, rr_b, rs_f, rr_f,
    ts_b, tr_b, ts_f, tr_f, os_b, or_b, os_f, or_f, zsem,
):
    p = lax.axis_index("pipe")
    e = lax.axis_index("expert")
    n_pipe = lax.axis_size("pipe")
    xq = e // NZ
    z = lax.rem(e, NZ)
    mine = xq // 2
    pair = (p, e + NZ - 2 * NZ * lax.rem(xq, 2))
    cross = (p, (3 - xq) * NZ + z)
    right = (p, e + 1)
    left = (p, e - 1)
    ahead = (p + 1, e)
    behind = (p - 1, e)
    has_l, has_r = z > 0, z < NZ - 1
    has_prev, has_next = p > 0, p < n_pipe - 1

    def remote(src, dst, ssem, rsem, dev):
        return pltpu.make_async_remote_copy(
            src_ref=src, dst_ref=dst, send_sem=ssem, recv_sem=rsem,
            device_id=dev, device_id_type=MESH,
        )

    loads = [
        pltpu.make_async_copy(xb_ref, xb_v, lsem.at[0]),
        pltpu.make_async_copy(dy_ref, dy_v, lsem.at[1]),
        pltpu.make_async_copy(x_ref, xf_v, lsem.at[2]),
        pltpu.make_async_copy(winb_ref.at[0, 0], wgu_b.at[0, :, pl.ds(0, HID)], lsem.at[3]),
        pltpu.make_async_copy(winb_ref.at[0, 1], wgu_b.at[0, :, pl.ds(HID, HID)], lsem.at[4]),
        pltpu.make_async_copy(wdb_ref.at[0], wd_b.at[pl.ds(0, HID)], lsem.at[5]),
        pltpu.make_async_copy(winf_ref.at[0, 0], wgu_f.at[0, :, pl.ds(0, HID)], lsem.at[6]),
        pltpu.make_async_copy(winf_ref.at[0, 1], wgu_f.at[0, :, pl.ds(HID, HID)], lsem.at[7]),
        pltpu.make_async_copy(wdf_ref.at[0], wd_f.at[pl.ds(0, HID)], lsem.at[8]),
    ]
    for c in loads:
        c.start()

    bar = pltpu.get_barrier_semaphore()

    def greet(dev):
        pl.semaphore_signal(bar, inc=1, device_id=dev, device_id_type=MESH)

    greet(pair)
    greet(cross)
    pl.when(has_l)(lambda: greet(left))
    pl.when(has_r)(lambda: greet(right))
    pl.when(has_prev)(lambda: greet(behind))
    pl.when(has_next)(lambda: greet(ahead))
    count = (
        2 + has_l.astype(jnp.int32) + has_r.astype(jnp.int32)
        + has_prev.astype(jnp.int32) + has_next.astype(jnp.int32)
    )
    pl.semaphore_wait(bar, count)

    weights = [
        remote(winb_ref.at[0, 0], wgu_b.at[1, :, pl.ds(0, HID)], ws.at[0], wr.at[0], pair),
        remote(winb_ref.at[0, 1], wgu_b.at[1, :, pl.ds(HID, HID)], ws.at[1], wr.at[1], pair),
        remote(wdb_ref.at[0], wd_b.at[pl.ds(HID, HID)], ws.at[2], wr.at[2], pair),
        remote(winf_ref.at[0, 0], wgu_f.at[1, :, pl.ds(0, HID)], ws.at[3], wr.at[3], pair),
        remote(winf_ref.at[0, 1], wgu_f.at[1, :, pl.ds(HID, HID)], ws.at[4], wr.at[4], pair),
        remote(wdf_ref.at[0], wd_f.at[pl.ds(HID, HID)], ws.at[5], wr.at[5], pair),
    ]
    for c in weights:
        c.start()

    def table(ids_ref, gate_ref, tg):
        ids = ids_ref[...]
        gate = gate_ref[...].astype(F32)
        lane = lax.broadcasted_iota(jnp.int32, (TOK, TOK), 1)
        row = lax.broadcasted_iota(jnp.int32, (TOK, TOK), 0)
        hits = jnp.zeros((TOK, TOK), F32)
        weight = jnp.zeros((TOK, TOK), F32)
        for i, expert in enumerate((mine, 1 - mine)):
            match = ids == expert
            hit = jnp.max(jnp.where(match, 1.0, 0.0), axis=1, keepdims=True)
            w = jnp.sum(jnp.where(match, gate, 0.0), axis=1, keepdims=True)
            here = (lane >= CAP * i) & (lane < CAP * (i + 1))
            hits = jnp.where(here, hit, hits)
            weight = jnp.where(here, w, weight)
        lower = jnp.where(row >= lane, 1.0, 0.0).astype(BF16)
        order = dot(lower, hits.astype(BF16))
        slot = ((lane & (CAP - 1)) + 1).astype(F32)
        tab = jnp.where(order == slot, hits, 0.0)
        tg[...] = (tab * weight).astype(BF16)[:, : 2 * CAP]
        return tab.T.astype(BF16)[: 2 * CAP]

    def normalise(src, gain_ref, keep):
        @pl.loop(0, TOK // 16)
        def _(i):
            rows = pl.ds(pl.multiple_of(i * 16, 16), 16)
            v = src[rows, :].astype(F32)
            r = lax.rsqrt(jnp.sum(v * v, axis=1, keepdims=True) * (1.0 / D) + EPS)
            xh[rows, :] = (v * r * gain_ref[...]).astype(BF16)
            if keep:
                rinv[rows, :] = jnp.broadcast_to(r, (16, TOK))

    def cols_of(c, width):
        return pl.ds(pl.multiple_of(c * width, width), width)

    def pick(tab, src, own_at, cross_at):
        @pl.loop(0, NC)
        def _(c):
            cols = cols_of(c, CW)
            s = dot(tab, src[:, cols]).astype(BF16)
            own_at(cols, s[:CAP])
            cross_at(cols, s[CAP:])

    def own_b(a):
        def put(cols, v):
            g_b[a, 2 * z, :, cols] = v
        return put

    def cross_b(a):
        def put(cols, v):
            x_b[a, :, cols] = v
        return put

    def own_f(cols, v):
        g_f[2 * z, :, cols] = v

    def cross_f(cols, v):
        x_f[:, cols] = v

    def gb_copy(b, way):
        return remote(
            g_b.at[:, b], g_b.at[:, b], gs_b.at[way, b], gr_b.at[b], (left, right)[way]
        )

    def gf_copy(b, way):
        return remote(g_f.at[b], g_f.at[b], gs_f.at[way, b], gr_f.at[b], (left, right)[way])

    def both_ways(copy, b):
        pl.when(has_r)(lambda: copy(b, 1).start())
        pl.when(has_l)(lambda: copy(b, 0).start())

    def gather_step(copy, k):
        for s in range(2):
            @pl.when(z >= k)
            def _():
                b = 2 * (z - k) + s
                copy(b, 1).wait_recv()
                pl.when(has_r)(lambda: copy(b, 1).start())

            @pl.when(z + k < NZ)
            def _():
                b = 2 * (z + k) + s
                copy(b, 0).wait_recv()
                pl.when(has_l)(lambda: copy(b, 0).start())

    def gather_drain(copy):
        for k in range(NZ):
            for s in range(2):
                @pl.when((z >= k) & has_r)
                def _():
                    copy(2 * (z - k) + s, 1).wait_send()

                @pl.when((z + k < NZ) & has_l)
                def _():
                    copy(2 * (z + k) + s, 0).wait_send()

    xb_copy = remote(x_b, g_b.at[:, 2 * z + 1], xs.at[0], gr_b.at[2 * z + 1], cross)
    xf_copy = remote(x_f, g_f.at[2 * z + 1], xs.at[1], gr_f.at[2 * z + 1], cross)

    tab = table(idb_ref, gb_ref, tg_b)
    loads[1].wait()
    pick(tab, dy_v, own_b(1), cross_b(1))
    loads[0].wait()
    normalise(xb_v, gainb_ref, True)
    pick(tab, xh, own_b(0), cross_b(0))
    xb_copy.start()
    both_ways(gb_copy, 2 * z)

    tab = table(idf_ref, gf_ref, tg_f)
    loads[2].wait()
    normalise(xf_v, gainf_ref, False)
    pick(tab, xh, own_f, cross_f)
    xf_copy.start()

    @pl.when(jnp.logical_not(has_prev))
    def _():
        @pl.loop(0, TOK // 16)
        def _(i):
            zero[pl.ds(pl.multiple_of(i * 16, 16), 16), :] = jnp.zeros((16, D), BF16)
        for i, out in enumerate((outf_ref, outb_ref)):
            pltpu.make_async_copy(zero, out, zsem.at[i]).start()

    xb_copy.wait_recv()
    both_ways(gb_copy, 2 * z + 1)
    gather_step(gb_copy, 1)
    gather_step(gb_copy, 2)
    both_ways(gf_copy, 2 * z)
    xf_copy.wait_recv()
    both_ways(gf_copy, 2 * z + 1)
    gather_step(gb_copy, 3)

    def reducer(part, got, ssem, rsem, chunked):
        def at(d, c):
            return (d, slice(None), cols_of(c, CW)) if chunked else (d,)

        def copy(d, way, c):
            i = (d, c) if chunked else (d,)
            return remote(
                part.at[at(d, c)], got.at[(1 - way,) + at(d, c)],
                ssem.at[i], rsem.at[(1 - way,) + i], (left, right)[way],
            )

        def add(d, side, c):
            if chunked:
                cols = cols_of(c, CW)
                part[d, :, cols] = (
                    part[d, :, cols].astype(F32) + got[side, d, :, cols].astype(F32)
                ).astype(BF16)
            else:
                pl.loop(0, NC)(lambda i: add_cols(d, side, cols_of(i, CW)))

        def add_cols(d, side, cols):
            part[d, :, cols] = (
                part[d, :, cols].astype(F32) + got[side, d, :, cols].astype(F32)
            ).astype(BF16)

        def edge(c):
            @pl.when(z == 0)
            def _():
                for d in range(NZ - 1, 0, -1):
                    copy(d, 1, c).start()

            @pl.when(z == NZ - 1)
            def _():
                for d in range(NZ - 1):
                    copy(d, 0, c).start()

        def relay(c, k):
            d = NZ - 1 - k

            @pl.when((z > 0) & (z < d))
            def _():
                copy(d, 1, c).wait_recv()
                add(d, 0, c)
                copy(d, 1, c).start()

            @pl.when((z < NZ - 1) & (z > k))
            def _():
                copy(k, 0, c).wait_recv()
                add(k, 1, c)
                copy(k, 0, c).start()

        def own(c):
            @pl.when(has_l)
            def _():
                copy(z, 1, c).wait_recv()
                add(z, 0, c)

            @pl.when(has_r)
            def _():
                copy(z, 0, c).wait_recv()
                add(z, 1, c)

        def drain(c):
            for d in range(NZ):
                pl.when(z < d)(lambda: copy(d, 1, c).wait_send())
                pl.when(z > d)(lambda: copy(d, 0, c).wait_send())

        return edge, relay, own, drain

    edge_b, relay_b, sum_b, drain_b = reducer(p_b, r_b, rs_b, rr_b, False)
    edge_f, relay_f, sum_f, drain_f = reducer(p_f, r_f, rs_f, rr_f, True)

    def totals_b():
        return remote(
            p_b.at[z, pl.ds(CAP, CAP)], tot_b, ts_b.at[0], tr_b.at[0], cross
        )

    def totals_f(c):
        cols = cols_of(c, CW)
        return remote(
            p_f.at[z, pl.ds(CAP, CAP), cols], tot_f.at[:, cols], ts_f.at[c], tr_f.at[c], cross
        )

    def shift_b():
        return remote(o_b, outb_ref, os_b.at[0], or_b.at[0], ahead)

    def shift_f(c):
        cols = cols_of(c, CW)
        return remote(o_f.at[:, cols], outf_ref.at[:, cols], os_f.at[c], or_f.at[c], ahead)

    for i in (3, 4, 5):
        loads[i].wait()
    for i in (0, 1, 2):
        weights[i].wait_recv()
    acc[...] = jnp.zeros_like(acc)
    accd[...] = jnp.zeros_like(accd)

    @pl.loop(0, D // KC)
    def _(c):
        cols = cols_of(c, KC)
        xs_c = g_b[0, :, :, cols].reshape(2 * NZ * CAP, KC)
        dy_c = g_b[1, :, :, cols].reshape(2 * NZ * CAP, KC)
        for o in range(2):
            acc[o] += dot(xs_c, wgu_b[o, cols, :])
        accd[...] += dot_t(dy_c, wd_b[:, cols])

    for o in range(2):
        a = acc[o, :, :HID]
        b = acc[o, :, HID:]
        dh = accd[:, o * HID : (o + 1) * HID]
        sg = jax.nn.sigmoid(a)
        hid[o, :, :HID] = (dh * b * sg * (1.0 + a * (1.0 - sg))).astype(BF16)
        hid[o, :, HID:] = (dh * a * sg).astype(BF16)

    @pl.loop(0, NC)
    def _(c):
        cols = cols_of(c, CW)
        part = dot_t(hid[0], wgu_b[0, cols, :]) + dot_t(hid[1], wgu_b[1, cols, :])
        p_b[:, :, cols] = part.astype(BF16).reshape(NZ, 2 * CAP, CW)

    edge_b(0)
    gather_step(gf_copy, 1)
    relay_b(0, 0)
    gather_step(gf_copy, 2)
    relay_b(0, 1)
    relay_b(0, 2)
    gather_step(gf_copy, 3)
    sum_b(0)
    totals_b().start()

    for i in (6, 7, 8):
        loads[i].wait()
    for i in (3, 4):
        weights[i].wait_recv()
    acc[...] = jnp.zeros_like(acc)

    @pl.loop(0, D // KC)
    def _(c):
        cols = cols_of(c, KC)
        xs_c = g_f[:, :, cols].reshape(2 * NZ * CAP, KC)
        for o in range(2):
            acc[o] += dot(xs_c, wgu_f[o, cols, :])

    for o in range(2):
        a = acc[o, :, :HID]
        hid[0, :, o * HID : (o + 1) * HID] = (
            a * jax.nn.sigmoid(a) * acc[o, :, HID:]
        ).astype(BF16)

    def finish_b():
        totals_b().wait_recv()

        def moe_cols(c, total):
            cols = cols_of(c, CW)
            rows = jnp.concatenate([p_b[z, pl.ds(0, CAP), cols], tot_b[:, cols]], axis=0)
            m = dot(tg_b[...], rows) * gainb_ref[:, cols]
            moe[:, cols] = m
            return total + jnp.sum(xb_v[:, cols].astype(F32) * m, axis=1, keepdims=True)

        total = lax.fori_loop(0, NC, moe_cols, jnp.zeros((TOK, 1), F32))
        r = rinv[:, :1]
        scale = r * r * r * (total * (1.0 / D))

        @pl.loop(0, NC)
        def _(c):
            cols = cols_of(c, CW)
            o_b[:, cols] = (
                dy_v[:, cols].astype(F32) + r * moe[:, cols] - xb_v[:, cols].astype(F32) * scale
            ).astype(BF16)

        pl.when(has_next)(lambda: shift_b().start())

    def part_f(c):
        cols = cols_of(c, CW)
        p_f[:, :, cols] = dot(hid[0], wd_f[:, cols]).astype(BF16).reshape(NZ, 2 * CAP, CW)

    def finish_f(c):
        totals_f(c).wait_recv()
        cols = cols_of(c, CW)
        rows = jnp.concatenate([p_f[z, pl.ds(0, CAP), cols], tot_f[:, cols]], axis=0)
        o_f[:, cols] = (xf_v[:, cols].astype(F32) + dot(tg_f[...], rows)).astype(BF16)
        pl.when(has_next)(lambda: shift_f(c).start())

    weights[5].wait_recv()

    @pl.loop(0, NC + 3)
    def _(i):
        @pl.when(i < NC)
        def _():
            part_f(i)
            edge_f(i)

        pl.when(i == 1)(finish_b)

        @pl.when((i >= 1) & (i < NC + 1))
        def _():
            for k in range(NZ - 1):
                relay_f(i - 1, k)

        @pl.when((i >= 2) & (i < NC + 2))
        def _():
            sum_f(i - 2)
            totals_f(i - 2).start()

        pl.when(i >= 3)(lambda: finish_f(i - 3))

    for c in weights:
        c.wait_send()
    xb_copy.wait_send()
    xf_copy.wait_send()
    gather_drain(gb_copy)
    gather_drain(gf_copy)
    drain_b(0)
    totals_b().wait_send()

    @pl.loop(0, NC)
    def _(c):
        drain_f(c)
        totals_f(c).wait_send()
        pl.when(has_next)(lambda: shift_f(c).wait_send())
        pl.when(has_prev)(lambda: shift_f(c).wait_recv())

    pl.when(has_next)(lambda: shift_b().wait_send())
    pl.when(has_prev)(lambda: shift_b().wait_recv())

    @pl.when(jnp.logical_not(has_prev))
    def _():
        for i, out in enumerate((outf_ref, outb_ref)):
            pltpu.make_async_copy(zero, out, zsem.at[i]).wait()


def local(*args):
    hbm = pl.BlockSpec(memory_space=pl.ANY)
    vmem = pl.BlockSpec(memory_space=pltpu.VMEM)
    dma = pltpu.SemaphoreType.DMA
    blocks = 2 * NZ
    rows = blocks * CAP
    return pl.pallas_call(
        kernel,
        out_shape=[jax.ShapeDtypeStruct((TOK, D), BF16)] * 2,
        in_specs=[
            hbm, vmem, vmem, vmem, hbm, hbm,
            hbm, hbm, vmem, vmem, vmem, hbm, hbm,
        ],
        out_specs=[hbm, hbm],
        scratch_shapes=[
            pltpu.VMEM((TOK, D), BF16),
            pltpu.VMEM((TOK, D), BF16),
            pltpu.VMEM((TOK, D), BF16),
            pltpu.VMEM((TOK, D), BF16),
            pltpu.VMEM((TOK, TOK), F32),
            pltpu.VMEM((TOK, 2 * CAP), BF16),
            pltpu.VMEM((TOK, 2 * CAP), BF16),
            pltpu.VMEM((2, D, 2 * HID), BF16),
            pltpu.VMEM((2 * HID, D), BF16),
            pltpu.VMEM((2, D, 2 * HID), BF16),
            pltpu.VMEM((2 * HID, D), BF16),
            pltpu.VMEM((2, blocks, CAP, D), BF16),
            pltpu.VMEM((blocks, CAP, D), BF16),
            pltpu.VMEM((2, CAP, D), BF16),
            pltpu.VMEM((CAP, D), BF16),
            pltpu.VMEM((NZ, 2 * CAP, D), BF16),
            pltpu.VMEM((NZ, 2 * CAP, D), BF16),
            pltpu.VMEM((2, NZ, 2 * CAP, D), BF16),
            pltpu.VMEM((2, NZ, 2 * CAP, D), BF16),
            pltpu.VMEM((CAP, D), BF16),
            pltpu.VMEM((CAP, D), BF16),
            pltpu.VMEM((2, rows, 2 * HID), F32),
            pltpu.VMEM((rows, 2 * HID), F32),
            pltpu.VMEM((2, rows, 2 * HID), BF16),
            pltpu.VMEM((TOK, D), F32),
            pltpu.VMEM((TOK, D), BF16),
            pltpu.VMEM((TOK, D), BF16),
            pltpu.VMEM((TOK, D), BF16),
            dma((9,)),
            dma((6,)),
            dma((6,)),
            dma((2, blocks)),
            dma((blocks,)),
            dma((2, blocks)),
            dma((blocks,)),
            dma((2,)),
            dma((NZ,)),
            dma((2, NZ)),
            dma((NZ, NC)),
            dma((2, NZ, NC)),
            dma((1,)),
            dma((1,)),
            dma((NC,)),
            dma((NC,)),
            dma((1,)),
            dma((1,)),
            dma((NC,)),
            dma((NC,)),
            dma((2,)),
        ],
        compiler_params=pltpu.CompilerParams(
            collective_id=0, has_side_effects=True, vmem_limit_bytes=56 * 2**20
        ),
        cost_estimate=pl.CostEstimate(
            flops=4 * 10**9, bytes_accessed=16 * 10**6, transcendentals=10**5
        ),
    )(*args)


def solution(mesh):
    tokens = P(("pipe", "expert"), None)
    w_in = P("pipe", None, None, "expert")
    w_down = P("pipe", "expert", None)
    gain = P("pipe", None)
    return jax.shard_map(
        local,
        mesh=mesh,
        in_specs=(
            tokens, tokens, tokens, gain, w_in, w_down,
            tokens, tokens, tokens, tokens, gain, w_in, w_down,
        ),
        out_specs=(tokens, tokens),
        check_vma=False,
    )
```

```python
import functools

import jax
import jax.numpy as jnp
from jax import lax
from jax.experimental import pallas as pl
from jax.experimental.pallas import tpu as pltpu
from jax.sharding import PartitionSpec as P

MESH = pl.DeviceIdType.MESH
F32 = jnp.float32
BF16 = jnp.bfloat16

D = 3584
CAP = 32
TOK = 128
HID = 128
NZ = 4
NC = 4
CW = D // NC
KC = 896
EPS = 1e-06
GAP = 0
ST = 1
FB = 0
TURN_AT = 2
W0_AT = 1
F_AT = (0, 1, 3)


def dot(a, b):
    return jnp.dot(a, b, preferred_element_type=F32)


def dot_t(a, b):
    return lax.dot_general(a, b, (((1,), (1,)), ((), ())), preferred_element_type=F32)


def kernel(
    x_ref, idf_ref, gf_ref, gainf_ref, winf_ref, wdf_ref,
    xb_ref, dy_ref, idb_ref, gb_ref, gainb_ref, winb_ref, wdb_ref,
    outf_ref, outb_ref,
    xf_v, xb_v, dy_v, xh, rinv, tg_f, tg_b,
    wgu_b, wd_b, wgu_f, wd_f,
    blk, crs, part, got, tot,
    acc, accd, hid, moe, o_b, o_f, zero,
    lsem, ws, wr, gs, gr, xs, rs, rr, ts, tr, os_b, or_b, os_f, or_f, zsem, turn,
):
    p = lax.axis_index("pipe")
    e = lax.axis_index("expert")
    n_pipe = lax.axis_size("pipe")
    xq = e // NZ
    z = lax.rem(e, NZ)
    mine = xq // 2
    pair = (p, e + NZ - 2 * NZ * lax.rem(xq, 2))
    cross = (p, (3 - xq) * NZ + z)
    right = (p, e + 1)
    left = (p, e - 1)
    ahead = (p + 1, e)
    behind = (p - 1, e)
    has_l, has_r = z > 0, z < NZ - 1
    has_prev, has_next = p > 0, p < n_pipe - 1
    first = lax.rem(p, 2) == 1

    def remote(src, dst, ssem, rsem, dev):
        return pltpu.make_async_remote_copy(
            src_ref=src, dst_ref=dst, send_sem=ssem, recv_sem=rsem,
            device_id=dev, device_id_type=MESH,
        )

    bar = pltpu.get_barrier_semaphore()

    def greet(dev):
        pl.semaphore_signal(bar, inc=1, device_id=dev, device_id_type=MESH)

    greet(pair)
    greet(cross)
    pl.when(has_l)(lambda: greet(left))
    pl.when(has_r)(lambda: greet(right))
    pl.when(has_prev)(lambda: greet(behind))
    pl.when(has_next)(lambda: greet(ahead))

    loads = [
        pltpu.make_async_copy(dy_ref, dy_v, lsem.at[0]),
        pltpu.make_async_copy(xb_ref, xb_v, lsem.at[1]),
        pltpu.make_async_copy(x_ref, xf_v, lsem.at[2]),
        pltpu.make_async_copy(winb_ref.at[0], wgu_b.at[0], lsem.at[3]),
        pltpu.make_async_copy(wdb_ref.at[0], wd_b.at[pl.ds(0, HID)], lsem.at[4]),
        pltpu.make_async_copy(winf_ref.at[0], wgu_f.at[0], lsem.at[5]),
        pltpu.make_async_copy(wdf_ref.at[0], wd_f.at[pl.ds(0, HID)], lsem.at[6]),
    ]
    for c in loads:
        c.start()

    def cols_of(c, width):
        return pl.ds(pl.multiple_of(c * width, width), width)

    def wd_copy(c):
        cols = cols_of(c, CW)
        return remote(
            wdf_ref.at[0, :, cols], wd_f.at[pl.ds(HID, HID), cols], ws.at[3 + c], wr.at[3 + c], pair
        )

    weights = [
        remote(winb_ref.at[0], wgu_b.at[1], ws.at[0], wr.at[0], pair),
        remote(wdb_ref.at[0], wd_b.at[pl.ds(HID, HID)], ws.at[1], wr.at[1], pair),
        remote(winf_ref.at[0], wgu_f.at[1], ws.at[2], wr.at[2], pair),
    ] + [wd_copy(c) for c in range(NC)]

    def table(ids_ref, gate_ref, tg):
        ids = ids_ref[...]
        gate = gate_ref[...].astype(F32)
        lane = lax.broadcasted_iota(jnp.int32, (TOK, TOK), 1)
        row = lax.broadcasted_iota(jnp.int32, (TOK, TOK), 0)
        hits = jnp.zeros((TOK, TOK), F32)
        weight = jnp.zeros((TOK, TOK), F32)
        for i, expert in enumerate((mine, 1 - mine)):
            match = ids == expert
            hit = jnp.max(jnp.where(match, 1.0, 0.0), axis=0, keepdims=True)
            w = jnp.sum(jnp.where(match, gate, 0.0), axis=0, keepdims=True)
            here = (row >= CAP * i) & (row < CAP * (i + 1))
            hits = jnp.where(here, hit, hits)
            weight = jnp.where(here, w, weight)
        upper = jnp.where(row <= lane, 1.0, 0.0).astype(BF16)
        order = dot(hits.astype(BF16), upper)
        slot = ((row & (CAP - 1)) + 1).astype(F32)
        tab = jnp.where(order == slot, hits, 0.0)
        tg[...] = (tab * weight).T.astype(BF16)[:, : 2 * CAP]
        return tab.astype(BF16)[: 2 * CAP]

    def normalise(src, gain_ref, keep):
        @pl.loop(0, TOK // 16)
        def _(i):
            rows = pl.ds(pl.multiple_of(i * 16, 16), 16)
            v = src[rows, :].astype(F32)
            r = lax.rsqrt(jnp.sum(v * v, axis=1, keepdims=True) * (1.0 / D) + EPS)
            xh[rows, :] = (v * r * gain_ref[...]).astype(BF16)
            if keep:
                rinv[rows, :] = jnp.broadcast_to(r, (16, TOK))

    def pick(tab, src, a):
        @pl.loop(0, NC)
        def _(c):
            cols = cols_of(c, CW)
            s = dot(tab, src[:, cols]).astype(BF16)
            blk[a, 2 * z, :, cols] = s[:CAP]
            crs[a, :, cols] = s[CAP:]

    def g_copy(a, b, way):
        return remote(
            blk.at[a, b], blk.at[a, b], gs.at[a, way, b], gr.at[a, b], (left, right)[way]
        )

    def x_copy(a):
        return remote(crs.at[a], blk.at[a, 2 * z + 1], xs.at[a], gr.at[a, 2 * z + 1], cross)

    def both_ways(a, b):
        pl.when(has_r)(lambda: g_copy(a, b, 1).start())
        pl.when(has_l)(lambda: g_copy(a, b, 0).start())

    def gather_step(arrays, k):
        for s in range(2):
            for a in arrays:
                @pl.when(z >= k)
                def _():
                    b = 2 * (z - k) + s
                    g_copy(a, b, 1).wait_recv()
                    pl.when(has_r)(lambda: g_copy(a, b, 1).start())

                @pl.when(z + k < NZ)
                def _():
                    b = 2 * (z + k) + s
                    g_copy(a, b, 0).wait_recv()
                    pl.when(has_l)(lambda: g_copy(a, b, 0).start())

    tab = table(idb_ref, gb_ref, tg_b)
    loads[0].wait()
    pick(tab, dy_v, 0)
    loads[1].wait()
    normalise(xb_v, gainb_ref, True)
    pick(tab, xh, 1)
    tab = table(idf_ref, gf_ref, tg_f)
    loads[2].wait()
    normalise(xf_v, gainf_ref, False)
    pick(tab, xh, 2)

    @pl.when(jnp.logical_not(has_prev))
    def _():
        @pl.loop(0, TOK // 16)
        def _(i):
            zero[pl.ds(pl.multiple_of(i * 16, 16), 16), :] = jnp.zeros((16, D), BF16)
        for i, out in enumerate((outf_ref, outb_ref)):
            pltpu.make_async_copy(zero, out, zsem.at[i]).start()

    pl.semaphore_wait(
        bar,
        2 + has_l.astype(jnp.int32) + has_r.astype(jnp.int32)
        + has_prev.astype(jnp.int32) + has_next.astype(jnp.int32),
    )

    second = jnp.logical_not(first)

    def start_weights():
        for c in weights:
            c.start()

    pl.when(first)(start_weights)
    if TURN_AT:
        pl.when(second)(lambda: pl.semaphore_wait(turn, 1))

    def give_turn(at):
        if TURN_AT == at:
            @pl.when(first)
            def _():
                pl.semaphore_signal(turn, inc=1, device_id=behind, device_id_type=MESH)
        if W0_AT == at:
            pl.when(second)(start_weights)

    if W0_AT == 0:
        pl.when(second)(start_weights)
    for a in range(2):
        x_copy(a).start()
        both_ways(a, 2 * z)
    x_copy(2).start()
    for a in range(2):
        x_copy(a).wait_recv()
        both_ways(a, 2 * z + 1)
    gather_step((0, 1), 1)
    give_turn(1)
    gather_step((0, 1), 2)
    give_turn(2)
    both_ways(2, 2 * z)
    x_copy(2).wait_recv()
    both_ways(2, 2 * z + 1)
    gather_step((0, 1), 3)
    give_turn(3)

    def split(g):
        return g // NC, cols_of(lax.rem(g, NC), CW)

    def r_copy(d, way, g):
        a, cols = split(g)
        return remote(
            part.at[a, d, :, cols], got.at[1 - way, a, d, :, cols],
            rs.at[g, d], rr.at[1 - way, g, d], (left, right)[way],
        )

    def add(d, side, g):
        a, cols = split(g)
        part[a, d, :, cols] = (
            part[a, d, :, cols].astype(F32) + got[side, a, d, :, cols].astype(F32)
        ).astype(BF16)

    def edge(g):
        @pl.when(z == 0)
        def _():
            for d in (3, 2, 1):
                r_copy(d, 1, g).start()

        @pl.when(z == NZ - 1)
        def _():
            for d in (0, 1, 2):
                r_copy(d, 0, g).start()

    def pass_on(d, way, g):
        r_copy(d, way, g).wait_recv()
        add(d, 1 - way, g)
        r_copy(d, way, g).start()

    def relay(g):
        @pl.when(z == 1)
        def _():
            pass_on(3, 1, g)
            pass_on(2, 1, g)

        @pl.when(z == 2)
        def _():
            pass_on(0, 0, g)
            pass_on(1, 0, g)

    def relay_again(g):
        pl.when(z == 1)(lambda: pass_on(0, 0, g))
        pl.when(z == 2)(lambda: pass_on(3, 1, g))

    def totals(g):
        a, cols = split(g)
        return remote(
            part.at[a, z, pl.ds(CAP, CAP), cols], tot.at[a, :, cols], ts.at[g], tr.at[g], cross
        )

    def own_sum(g):
        @pl.when(has_l)
        def _():
            r_copy(z, 1, g).wait_recv()
            add(z, 0, g)

        @pl.when(has_r)
        def _():
            r_copy(z, 0, g).wait_recv()
            add(z, 1, g)

        totals(g).start()

    def total_rows(a, cols):
        return jnp.concatenate([part[a, z, pl.ds(0, CAP), cols], tot[a, :, cols]], axis=0)

    def shift_b():
        return remote(o_b, outb_ref, os_b.at[0], or_b.at[0], ahead)

    def shift_f(c):
        cols = cols_of(c, CW)
        return remote(o_f.at[:, cols], outf_ref.at[:, cols], os_f.at[c], or_f.at[c], ahead)

    for i in (3, 4):
        loads[i].wait()
    for i in (0, 1):
        weights[i].wait_recv()
    acc[...] = jnp.zeros_like(acc)
    accd[...] = jnp.zeros_like(accd)

    def gate_up(w, o, rows):
        return jnp.concatenate([w[o, 0, rows, :], w[o, 1, rows, :]], axis=1)

    @pl.loop(0, D // KC)
    def _(c):
        cols = cols_of(c, KC)
        xs_c = blk[1, :, :, cols].reshape(2 * NZ * CAP, KC)
        dy_c = blk[0, :, :, cols].reshape(2 * NZ * CAP, KC)
        for o in range(2):
            acc[o] += dot(xs_c, gate_up(wgu_b, o, cols))
        accd[...] += dot_t(dy_c, wd_b[:, cols])

    for o in range(2):
        a = acc[o, :, :HID]
        b = acc[o, :, HID:]
        dh = accd[:, o * HID : (o + 1) * HID]
        sg = jax.nn.sigmoid(a)
        hid[o, :, :HID] = (dh * b * sg * (1.0 + a * (1.0 - sg))).astype(BF16)
        hid[o, :, HID:] = (dh * a * sg).astype(BF16)

    def part_b(c):
        cols = cols_of(c, CW)
        v = dot_t(hid[0], gate_up(wgu_b, 0, cols)) + dot_t(hid[1], gate_up(wgu_b, 1, cols))
        part[0, :, :, cols] = v.astype(BF16).reshape(NZ, 2 * CAP, CW)

    def hidden_f():
        for i in (5, 6):
            loads[i].wait()
        weights[2].wait_recv()
        acc[...] = jnp.zeros_like(acc)

        @pl.loop(0, D // KC)
        def _(c):
            cols = cols_of(c, KC)
            xs_c = blk[2, :, :, cols].reshape(2 * NZ * CAP, KC)
            for o in range(2):
                acc[o] += dot(xs_c, gate_up(wgu_f, o, cols))

        for o in range(2):
            a = acc[o, :, :HID]
            hid[0, :, o * HID : (o + 1) * HID] = (
                a * jax.nn.sigmoid(a) * acc[o, :, HID:]
            ).astype(BF16)

    def part_f(c):
        wd_copy(c).wait_recv()
        cols = cols_of(c, CW)
        v = dot(hid[0], wd_f[:, cols])
        part[1, :, :, cols] = v.astype(BF16).reshape(NZ, 2 * CAP, CW)

    def finish_b():
        pl.loop(0, NC)(lambda c: totals(c).wait_recv())

        def moe_cols(c, total):
            cols = cols_of(c, CW)
            m = dot(tg_b[...], total_rows(0, cols)) * gainb_ref[:, cols]
            moe[:, cols] = m
            return total + jnp.sum(xb_v[:, cols].astype(F32) * m, axis=1, keepdims=True)

        total = lax.fori_loop(0, NC, moe_cols, jnp.zeros((TOK, 1), F32))
        r = rinv[:, :1]
        scale = r * r * r * (total * (1.0 / D))

        @pl.loop(0, NC)
        def _(c):
            cols = cols_of(c, CW)
            o_b[:, cols] = (
                dy_v[:, cols].astype(F32) + r * moe[:, cols] - xb_v[:, cols].astype(F32) * scale
            ).astype(BF16)

        pl.when(has_next)(lambda: shift_b().start())

    def finish_f(c):
        totals(NC + c).wait_recv()
        cols = cols_of(c, CW)
        o_f[:, cols] = (
            xf_v[:, cols].astype(F32) + dot(tg_f[...], total_rows(1, cols))
        ).astype(BF16)
        pl.when(has_next)(lambda: shift_f(c).start())

    @pl.loop(0, 2 * NC + GAP + 4 * ST)
    def _(i):
        def stage(late, f):
            j = i - late
            back = (j >= 0) & (j < NC)
            front = (j >= NC + GAP) & (j < 2 * NC + GAP)
            pl.when(back | front)(lambda: f(j - GAP * front.astype(jnp.int32)))

        pl.when(i == NC + GAP)(hidden_f)
        pl.when(i < NC)(lambda: part_b(i))
        pl.when((i >= NC + GAP) & (i < 2 * NC + GAP))(lambda: part_f(i - NC - GAP))
        stage(0, edge)
        for k in range(1, NZ):
            pl.when(i == F_AT[k - 1])(lambda: gather_step((2,), k))
        stage(ST, relay)
        stage(2 * ST, relay_again)
        stage(3 * ST, own_sum)
        pl.when(i == NC + 3 * ST + FB)(finish_b)
        pl.when(i >= NC + GAP + 4 * ST)(lambda: finish_f(i - NC - GAP - 4 * ST))

    for c in weights:
        c.wait_send()
    for a in range(3):
        x_copy(a).wait_send()
        for k in range(NZ):
            for s in range(2):
                @pl.when((z >= k) & has_r)
                def _():
                    g_copy(a, 2 * (z - k) + s, 1).wait_send()

                @pl.when((z + k < NZ) & has_l)
                def _():
                    g_copy(a, 2 * (z + k) + s, 0).wait_send()

    @pl.loop(0, 2 * NC)
    def _(g):
        for d in range(NZ):
            pl.when(z < d)(lambda: r_copy(d, 1, g).wait_send())
            pl.when(z > d)(lambda: r_copy(d, 0, g).wait_send())
        totals(g).wait_send()

    @pl.loop(0, NC)
    def _(c):
        pl.when(has_next)(lambda: shift_f(c).wait_send())
        pl.when(has_prev)(lambda: shift_f(c).wait_recv())

    pl.when(has_next)(lambda: shift_b().wait_send())
    pl.when(has_prev)(lambda: shift_b().wait_recv())

    @pl.when(jnp.logical_not(has_prev))
    def _():
        for i, out in enumerate((outf_ref, outb_ref)):
            pltpu.make_async_copy(zero, out, zsem.at[i]).wait()


def local(x, idf, gf, gainf, winf, wdf, xb, dy, idb, gb, gainb, winb, wdb):
    hbm = pl.BlockSpec(memory_space=pl.ANY)
    vmem = pl.BlockSpec(memory_space=pltpu.VMEM)
    dma = pltpu.SemaphoreType.DMA
    blocks = 2 * NZ
    rows = blocks * CAP
    return pl.pallas_call(
        kernel,
        out_shape=[jax.ShapeDtypeStruct((TOK, D), BF16)] * 2,
        in_specs=[
            hbm, vmem, vmem, vmem, hbm, hbm,
            hbm, hbm, vmem, vmem, vmem, hbm, hbm,
        ],
        out_specs=[hbm, hbm],
        scratch_shapes=[
            pltpu.VMEM((TOK, D), BF16),
            pltpu.VMEM((TOK, D), BF16),
            pltpu.VMEM((TOK, D), BF16),
            pltpu.VMEM((TOK, D), BF16),
            pltpu.VMEM((TOK, TOK), F32),
            pltpu.VMEM((TOK, 2 * CAP), BF16),
            pltpu.VMEM((TOK, 2 * CAP), BF16),
            pltpu.VMEM((2, 2, D, HID), BF16),
            pltpu.VMEM((2 * HID, D), BF16),
            pltpu.VMEM((2, 2, D, HID), BF16),
            pltpu.VMEM((2 * HID, D), BF16),
            pltpu.VMEM((3, blocks, CAP, D), BF16),
            pltpu.VMEM((3, CAP, D), BF16),
            pltpu.VMEM((2, NZ, 2 * CAP, D), BF16),
            pltpu.VMEM((2, 2, NZ, 2 * CAP, D), BF16),
            pltpu.VMEM((2, CAP, D), BF16),
            pltpu.VMEM((2, rows, 2 * HID), F32),
            pltpu.VMEM((rows, 2 * HID), F32),
            pltpu.VMEM((2, rows, 2 * HID), BF16),
            pltpu.VMEM((TOK, D), F32),
            pltpu.VMEM((TOK, D), BF16),
            pltpu.VMEM((TOK, D), BF16),
            pltpu.VMEM((TOK, D), BF16),
            dma((7,)),
            dma((3 + NC,)),
            dma((3 + NC,)),
            dma((3, 2, blocks)),
            dma((3, blocks)),
            dma((3,)),
            dma((2 * NC, NZ)),
            dma((2, 2 * NC, NZ)),
            dma((2 * NC,)),
            dma((2 * NC,)),
            dma((1,)),
            dma((1,)),
            dma((NC,)),
            dma((NC,)),
            dma((2,)),
            pltpu.SemaphoreType.REGULAR,
        ],
        compiler_params=pltpu.CompilerParams(
            collective_id=0, has_side_effects=True, vmem_limit_bytes=56 * 2**20
        ),
        cost_estimate=pl.CostEstimate(
            flops=4 * 10**9, bytes_accessed=16 * 10**6, transcendentals=10**5
        ),
    )(x, idf.T, gf.T, gainf, winf, wdf, xb, dy, idb.T, gb.T, gainb, winb, wdb)


def solution(mesh):
    tokens = P(("pipe", "expert"), None)
    w_in = P("pipe", None, None, "expert")
    w_down = P("pipe", "expert", None)
    gain = P("pipe", None)
    return jax.shard_map(
        local,
        mesh=mesh,
        in_specs=(
            tokens, tokens, tokens, gain, w_in, w_down,
            tokens, tokens, tokens, tokens, gain, w_in, w_down,
        ),
        out_specs=(tokens, tokens),
        check_vma=False,
    )
```

```python
import functools

import jax
import jax.numpy as jnp
from jax import lax
from jax.experimental import pallas as pl
from jax.experimental.pallas import tpu as pltpu
from jax.sharding import PartitionSpec as P

MESH = pl.DeviceIdType.MESH
F32 = jnp.float32
BF16 = jnp.bfloat16

D = 3584
CAP = 32
TOK = 128
HID = 128
NZ = 4
NC = 4
CW = D // NC
KC = 896
EPS = 1e-06
GAP = 0
ST = 1
FB = 0
TURN_AT = 2
W0_AT = 1
F_AT = (0, 1, 3)


def dot(a, b):
    return jnp.dot(a, b, preferred_element_type=F32)


def dot_t(a, b):
    return lax.dot_general(a, b, (((1,), (1,)), ((), ())), preferred_element_type=F32)


def kernel(
    x_ref, idf_ref, gf_ref, gainf_ref, winf_ref, wdf_ref,
    xb_ref, dy_ref, idb_ref, gb_ref, gainb_ref, winb_ref, wdb_ref,
    outf_ref, outb_ref,
    xf_v, xb_v, dy_v, xh, rinv, tg_f, tg_b,
    wgu_b, wd_b, wgu_f, wd_f,
    blk, crs, part, got, tot,
    acc, accd, hid, moe, o_b, o_f, zero,
    lsem, ws, wr, gs, gr, xs, rs, rr, ts, tr, os_b, or_b, os_f, or_f, zsem, turn,
):
    p = lax.axis_index("pipe")
    e = lax.axis_index("expert")
    n_pipe = lax.axis_size("pipe")
    xq = e // NZ
    z = lax.rem(e, NZ)
    mine = xq // 2
    pair = (p, e + NZ - 2 * NZ * lax.rem(xq, 2))
    cross = (p, (3 - xq) * NZ + z)
    right = (p, e + 1)
    left = (p, e - 1)
    ahead = (p + 1, e)
    behind = (p - 1, e)
    has_l, has_r = z > 0, z < NZ - 1
    has_prev, has_next = p > 0, p < n_pipe - 1
    first = lax.rem(p, 2) == 1

    def remote(src, dst, ssem, rsem, dev):
        return pltpu.make_async_remote_copy(
            src_ref=src, dst_ref=dst, send_sem=ssem, recv_sem=rsem,
            device_id=dev, device_id_type=MESH,
        )

    bar = pltpu.get_barrier_semaphore()

    def greet(dev):
        pl.semaphore_signal(bar, inc=1, device_id=dev, device_id_type=MESH)

    greet(pair)
    greet(cross)
    pl.when(has_l)(lambda: greet(left))
    pl.when(has_r)(lambda: greet(right))
    pl.when(has_prev)(lambda: greet(behind))
    pl.when(has_next)(lambda: greet(ahead))

    loads = [
        pltpu.make_async_copy(dy_ref, dy_v, lsem.at[0]),
        pltpu.make_async_copy(xb_ref, xb_v, lsem.at[1]),
        pltpu.make_async_copy(x_ref, xf_v, lsem.at[2]),
        pltpu.make_async_copy(winb_ref.at[0], wgu_b.at[0], lsem.at[3]),
        pltpu.make_async_copy(wdb_ref.at[0], wd_b.at[pl.ds(0, HID)], lsem.at[4]),
        pltpu.make_async_copy(winf_ref.at[0], wgu_f.at[0], lsem.at[5]),
        pltpu.make_async_copy(wdf_ref.at[0], wd_f.at[pl.ds(0, HID)], lsem.at[6]),
    ]
    for c in loads:
        c.start()

    def cols_of(c, width):
        return pl.ds(pl.multiple_of(c * width, width), width)

    def wd_copy(c):
        cols = cols_of(c, CW)
        return remote(
            wdf_ref.at[0, :, cols], wd_f.at[pl.ds(HID, HID), cols], ws.at[3 + c], wr.at[3 + c], pair
        )

    weights = [
        remote(winb_ref.at[0], wgu_b.at[1], ws.at[0], wr.at[0], pair),
        remote(wdb_ref.at[0], wd_b.at[pl.ds(HID, HID)], ws.at[1], wr.at[1], pair),
        remote(winf_ref.at[0], wgu_f.at[1], ws.at[2], wr.at[2], pair),
    ] + [wd_copy(c) for c in range(NC)]

    def table(ids_ref, gate_ref, tg):
        ids = ids_ref[...]
        gate = gate_ref[...].astype(F32)
        lane = lax.broadcasted_iota(jnp.int32, (TOK, TOK), 1)
        row = lax.broadcasted_iota(jnp.int32, (TOK, TOK), 0)
        hits = jnp.zeros((TOK, TOK), F32)
        weight = jnp.zeros((TOK, TOK), F32)
        for i, expert in enumerate((mine, 1 - mine)):
            match = ids == expert
            hit = jnp.max(jnp.where(match, 1.0, 0.0), axis=0, keepdims=True)
            w = jnp.sum(jnp.where(match, gate, 0.0), axis=0, keepdims=True)
            here = (row >= CAP * i) & (row < CAP * (i + 1))
            hits = jnp.where(here, hit, hits)
            weight = jnp.where(here, w, weight)
        upper = jnp.where(row <= lane, 1.0, 0.0).astype(BF16)
        order = dot(hits.astype(BF16), upper)
        slot = ((row & (CAP - 1)) + 1).astype(F32)
        tab = jnp.where(order == slot, hits, 0.0)
        tg[...] = (tab * weight).T.astype(BF16)[:, : 2 * CAP]
        return tab.astype(BF16)[: 2 * CAP]

    def normalise(src, gain_ref, keep):
        @pl.loop(0, TOK // 16)
        def _(i):
            rows = pl.ds(pl.multiple_of(i * 16, 16), 16)
            v = src[rows, :].astype(F32)
            r = lax.rsqrt(jnp.sum(v * v, axis=1, keepdims=True) * (1.0 / D) + EPS)
            xh[rows, :] = (v * r * gain_ref[...]).astype(BF16)
            if keep:
                rinv[rows, :] = jnp.broadcast_to(r, (16, TOK))

    def pick(tab, src, a):
        @pl.loop(0, NC)
        def _(c):
            cols = cols_of(c, CW)
            s = dot(tab, src[:, cols]).astype(BF16)
            blk[a, 2 * z, :, cols] = s[:CAP]
            crs[a, :, cols] = s[CAP:]

    def g_copy(a, b, way):
        return remote(
            blk.at[a, b], blk.at[a, b], gs.at[a, way, b], gr.at[a, b], (left, right)[way]
        )

    def x_copy(a):
        return remote(crs.at[a], blk.at[a, 2 * z + 1], xs.at[a], gr.at[a, 2 * z + 1], cross)

    def both_ways(a, b):
        pl.when(has_r)(lambda: g_copy(a, b, 1).start())
        pl.when(has_l)(lambda: g_copy(a, b, 0).start())

    def gather_step(arrays, k):
        for s in range(2):
            for a in arrays:
                @pl.when(z >= k)
                def _():
                    b = 2 * (z - k) + s
                    g_copy(a, b, 1).wait_recv()
                    pl.when(has_r)(lambda: g_copy(a, b, 1).start())

                @pl.when(z + k < NZ)
                def _():
                    b = 2 * (z + k) + s
                    g_copy(a, b, 0).wait_recv()
                    pl.when(has_l)(lambda: g_copy(a, b, 0).start())

    tab = table(idb_ref, gb_ref, tg_b)
    loads[0].wait()
    pick(tab, dy_v, 0)
    loads[1].wait()
    normalise(xb_v, gainb_ref, True)
    pick(tab, xh, 1)
    tab = table(idf_ref, gf_ref, tg_f)
    loads[2].wait()
    normalise(xf_v, gainf_ref, False)
    pick(tab, xh, 2)

    @pl.when(jnp.logical_not(has_prev))
    def _():
        @pl.loop(0, TOK // 16)
        def _(i):
            zero[pl.ds(pl.multiple_of(i * 16, 16), 16), :] = jnp.zeros((16, D), BF16)
        for i, out in enumerate((outf_ref, outb_ref)):
            pltpu.make_async_copy(zero, out, zsem.at[i]).start()

    pl.semaphore_wait(
        bar,
        2 + has_l.astype(jnp.int32) + has_r.astype(jnp.int32)
        + has_prev.astype(jnp.int32) + has_next.astype(jnp.int32),
    )

    second = jnp.logical_not(first)

    def start_weights():
        for c in weights:
            c.start()

    pl.when(first)(start_weights)
    if TURN_AT:
        pl.when(second)(lambda: pl.semaphore_wait(turn, 1))

    def give_turn(at):
        if TURN_AT == at:
            @pl.when(first)
            def _():
                pl.semaphore_signal(turn, inc=1, device_id=behind, device_id_type=MESH)
        if W0_AT == at:
            pl.when(second)(start_weights)

    if W0_AT == 0:
        pl.when(second)(start_weights)
    for a in range(2):
        x_copy(a).start()
        both_ways(a, 2 * z)
    x_copy(2).start()
    for a in range(2):
        x_copy(a).wait_recv()
        both_ways(a, 2 * z + 1)
    gather_step((0, 1), 1)
    give_turn(1)
    gather_step((0, 1), 2)
    give_turn(2)
    both_ways(2, 2 * z)
    x_copy(2).wait_recv()
    both_ways(2, 2 * z + 1)
    gather_step((0, 1), 3)
    give_turn(3)

    def split(g):
        return g // NC, cols_of(lax.rem(g, NC), CW)

    def r_copy(d, way, g):
        a, cols = split(g)
        return remote(
            part.at[a, d, :, cols], got.at[1 - way, a, d, :, cols],
            rs.at[g, d], rr.at[1 - way, g, d], (left, right)[way],
        )

    def add(d, side, g):
        a, cols = split(g)
        part[a, d, :, cols] = (
            part[a, d, :, cols].astype(F32) + got[side, a, d, :, cols].astype(F32)
        ).astype(BF16)

    def edge(g):
        @pl.when(z == 0)
        def _():
            for d in (3, 2, 1):
                r_copy(d, 1, g).start()

        @pl.when(z == NZ - 1)
        def _():
            for d in (0, 1, 2):
                r_copy(d, 0, g).start()

    def pass_on(d, way, g):
        r_copy(d, way, g).wait_recv()
        add(d, 1 - way, g)
        r_copy(d, way, g).start()

    def relay(g):
        @pl.when(z == 1)
        def _():
            pass_on(3, 1, g)
            pass_on(2, 1, g)

        @pl.when(z == 2)
        def _():
            pass_on(0, 0, g)
            pass_on(1, 0, g)

    def relay_again(g):
        pl.when(z == 1)(lambda: pass_on(0, 0, g))
        pl.when(z == 2)(lambda: pass_on(3, 1, g))

    def totals(g):
        a, cols = split(g)
        return remote(
            part.at[a, z, pl.ds(CAP, CAP), cols], tot.at[a, :, cols], ts.at[g], tr.at[g], cross
        )

    def own_sum(g):
        @pl.when(has_l)
        def _():
            r_copy(z, 1, g).wait_recv()
            add(z, 0, g)

        @pl.when(has_r)
        def _():
            r_copy(z, 0, g).wait_recv()
            add(z, 1, g)

        totals(g).start()

    def total_rows(a, cols):
        return jnp.concatenate([part[a, z, pl.ds(0, CAP), cols], tot[a, :, cols]], axis=0)

    def shift_b():
        return remote(o_b, outb_ref, os_b.at[0], or_b.at[0], ahead)

    def shift_f(c):
        cols = cols_of(c, CW)
        return remote(o_f.at[:, cols], outf_ref.at[:, cols], os_f.at[c], or_f.at[c], ahead)

    for i in (3, 4):
        loads[i].wait()
    for i in (0, 1):
        weights[i].wait_recv()
    acc[...] = jnp.zeros_like(acc)
    accd[...] = jnp.zeros_like(accd)

    def gate_up(w, o, rows):
        return jnp.concatenate([w[o, 0, rows, :], w[o, 1, rows, :]], axis=1)

    @pl.loop(0, D // KC)
    def _(c):
        cols = cols_of(c, KC)
        xs_c = blk[1, :, :, cols].reshape(2 * NZ * CAP, KC)
        dy_c = blk[0, :, :, cols].reshape(2 * NZ * CAP, KC)
        for o in range(2):
            acc[o] += dot(xs_c, gate_up(wgu_b, o, cols))
        accd[...] += dot_t(dy_c, wd_b[:, cols])

    for o in range(2):
        a = acc[o, :, :HID]
        b = acc[o, :, HID:]
        dh = accd[:, o * HID : (o + 1) * HID]
        sg = jax.nn.sigmoid(a)
        hid[o, :, :HID] = (dh * b * sg * (1.0 + a * (1.0 - sg))).astype(BF16)
        hid[o, :, HID:] = (dh * a * sg).astype(BF16)

    def part_b(c):
        cols = cols_of(c, CW)
        v = dot_t(hid[0], gate_up(wgu_b, 0, cols)) + dot_t(hid[1], gate_up(wgu_b, 1, cols))
        part[0, :, :, cols] = v.astype(BF16).reshape(NZ, 2 * CAP, CW)

    def hidden_f():
        for i in (5, 6):
            loads[i].wait()
        acc[...] = jnp.zeros_like(acc)

        for o in range(2):
            if o == 1:
                weights[2].wait_recv()

            @pl.loop(0, D // KC)
            def _(c):
                cols = cols_of(c, KC)
                xs_c = blk[2, :, :, cols].reshape(2 * NZ * CAP, KC)
                acc[o] += dot(xs_c, gate_up(wgu_f, o, cols))

            a = acc[o, :, :HID]
            hid[0, :, o * HID : (o + 1) * HID] = (
                a * jax.nn.sigmoid(a) * acc[o, :, HID:]
            ).astype(BF16)

    def part_f(c):
        wd_copy(c).wait_recv()
        cols = cols_of(c, CW)
        v = dot(hid[0], wd_f[:, cols])
        part[1, :, :, cols] = v.astype(BF16).reshape(NZ, 2 * CAP, CW)

    def finish_b():
        pl.loop(0, NC)(lambda c: totals(c).wait_recv())

        def moe_cols(c, total):
            cols = cols_of(c, CW)
            m = dot(tg_b[...], total_rows(0, cols)) * gainb_ref[:, cols]
            moe[:, cols] = m
            return total + jnp.sum(xb_v[:, cols].astype(F32) * m, axis=1, keepdims=True)

        total = lax.fori_loop(0, NC, moe_cols, jnp.zeros((TOK, 1), F32))
        r = rinv[:, :1]
        scale = r * r * r * (total * (1.0 / D))

        @pl.loop(0, NC)
        def _(c):
            cols = cols_of(c, CW)
            o_b[:, cols] = (
                dy_v[:, cols].astype(F32) + r * moe[:, cols] - xb_v[:, cols].astype(F32) * scale
            ).astype(BF16)

        pl.when(has_next)(lambda: shift_b().start())

    def finish_f(c):
        totals(NC + c).wait_recv()
        cols = cols_of(c, CW)
        o_f[:, cols] = (
            xf_v[:, cols].astype(F32) + dot(tg_f[...], total_rows(1, cols))
        ).astype(BF16)
        pl.when(has_next)(lambda: shift_f(c).start())

    @pl.loop(0, 2 * NC + GAP + 4 * ST)
    def _(i):
        def stage(late, f):
            j = i - late
            back = (j >= 0) & (j < NC)
            front = (j >= NC + GAP) & (j < 2 * NC + GAP)
            pl.when(back | front)(lambda: f(j - GAP * front.astype(jnp.int32)))

        pl.when(i == NC + GAP)(hidden_f)
        pl.when(i < NC)(lambda: part_b(i))
        pl.when((i >= NC + GAP) & (i < 2 * NC + GAP))(lambda: part_f(i - NC - GAP))
        stage(0, edge)
        for k in range(1, NZ):
            pl.when(i == F_AT[k - 1])(lambda: gather_step((2,), k))
        stage(ST, relay)
        stage(2 * ST, relay_again)
        stage(3 * ST, own_sum)
        pl.when(i == NC + 3 * ST + FB)(finish_b)
        pl.when(i >= NC + GAP + 4 * ST)(lambda: finish_f(i - NC - GAP - 4 * ST))

    for c in weights:
        c.wait_send()
    for a in range(3):
        x_copy(a).wait_send()
        for k in range(NZ):
            for s in range(2):
                @pl.when((z >= k) & has_r)
                def _():
                    g_copy(a, 2 * (z - k) + s, 1).wait_send()

                @pl.when((z + k < NZ) & has_l)
                def _():
                    g_copy(a, 2 * (z + k) + s, 0).wait_send()

    @pl.loop(0, 2 * NC)
    def _(g):
        for d in range(NZ):
            pl.when(z < d)(lambda: r_copy(d, 1, g).wait_send())
            pl.when(z > d)(lambda: r_copy(d, 0, g).wait_send())
        totals(g).wait_send()

    @pl.loop(0, NC)
    def _(c):
        pl.when(has_next)(lambda: shift_f(c).wait_send())
        pl.when(has_prev)(lambda: shift_f(c).wait_recv())

    pl.when(has_next)(lambda: shift_b().wait_send())
    pl.when(has_prev)(lambda: shift_b().wait_recv())

    @pl.when(jnp.logical_not(has_prev))
    def _():
        for i, out in enumerate((outf_ref, outb_ref)):
            pltpu.make_async_copy(zero, out, zsem.at[i]).wait()


def local(x, idf, gf, gainf, winf, wdf, xb, dy, idb, gb, gainb, winb, wdb):
    hbm = pl.BlockSpec(memory_space=pl.ANY)
    vmem = pl.BlockSpec(memory_space=pltpu.VMEM)
    dma = pltpu.SemaphoreType.DMA
    blocks = 2 * NZ
    rows = blocks * CAP
    return pl.pallas_call(
        kernel,
        out_shape=[jax.ShapeDtypeStruct((TOK, D), BF16)] * 2,
        in_specs=[
            hbm, vmem, vmem, vmem, hbm, hbm,
            hbm, hbm, vmem, vmem, vmem, hbm, hbm,
        ],
        out_specs=[hbm, hbm],
        scratch_shapes=[
            pltpu.VMEM((TOK, D), BF16),
            pltpu.VMEM((TOK, D), BF16),
            pltpu.VMEM((TOK, D), BF16),
            pltpu.VMEM((TOK, D), BF16),
            pltpu.VMEM((TOK, TOK), F32),
            pltpu.VMEM((TOK, 2 * CAP), BF16),
            pltpu.VMEM((TOK, 2 * CAP), BF16),
            pltpu.VMEM((2, 2, D, HID), BF16),
            pltpu.VMEM((2 * HID, D), BF16),
            pltpu.VMEM((2, 2, D, HID), BF16),
            pltpu.VMEM((2 * HID, D), BF16),
            pltpu.VMEM((3, blocks, CAP, D), BF16),
            pltpu.VMEM((3, CAP, D), BF16),
            pltpu.VMEM((2, NZ, 2 * CAP, D), BF16),
            pltpu.VMEM((2, 2, NZ, 2 * CAP, D), BF16),
            pltpu.VMEM((2, CAP, D), BF16),
            pltpu.VMEM((2, rows, 2 * HID), F32),
            pltpu.VMEM((rows, 2 * HID), F32),
            pltpu.VMEM((2, rows, 2 * HID), BF16),
            pltpu.VMEM((TOK, D), F32),
            pltpu.VMEM((TOK, D), BF16),
            pltpu.VMEM((TOK, D), BF16),
            pltpu.VMEM((TOK, D), BF16),
            dma((7,)),
            dma((3 + NC,)),
            dma((3 + NC,)),
            dma((3, 2, blocks)),
            dma((3, blocks)),
            dma((3,)),
            dma((2 * NC, NZ)),
            dma((2, 2 * NC, NZ)),
            dma((2 * NC,)),
            dma((2 * NC,)),
            dma((1,)),
            dma((1,)),
            dma((NC,)),
            dma((NC,)),
            dma((2,)),
            pltpu.SemaphoreType.REGULAR,
        ],
        compiler_params=pltpu.CompilerParams(
            collective_id=0, has_side_effects=True, vmem_limit_bytes=56 * 2**20
        ),
        cost_estimate=pl.CostEstimate(
            flops=4 * 10**9, bytes_accessed=16 * 10**6, transcendentals=10**5
        ),
    )(x, idf.T, gf.T, gainf, winf, wdf, xb, dy, idb.T, gb.T, gainb, winb, wdb)


def solution(mesh):
    tokens = P(("pipe", "expert"), None)
    w_in = P("pipe", None, None, "expert")
    w_down = P("pipe", "expert", None)
    gain = P("pipe", None)
    return jax.shard_map(
        local,
        mesh=mesh,
        in_specs=(
            tokens, tokens, tokens, gain, w_in, w_down,
            tokens, tokens, tokens, tokens, gain, w_in, w_down,
        ),
        out_specs=(tokens, tokens),
        check_vma=False,
    )
```
